32 devices in a mesh: inp: 4 (over z), tm: 4 (over y, x), bl: 2 (over core).
Axes of the slice: x: 2, y: 2, z: 4, core: 2. Of those that a mesh axis runs over, the one named last changes fastest.
Arguments:
- voltages: int32 [1024, 262144], P(('inp', 'bl'), 'tm'), may hold values from -16 to 14, as said below
- taps: float32 [4, 16384], replicated, may hold values from -3 to 3
- flags: int32 [1024], P(('inp', 'bl')), may hold values 0 or 1
Outputs:
- visibilities: float32 [2, 128, 4, 256, 1024], P(None, ('inp', 'tm'), None, 'bl')
The draws below stay inside these ranges and needn't reach their ends.
Inputs may be any that keep to these rules, and one draw needn't show every extreme that they name: `voltages`: int8-valued digitized samples, each input's stream in time order.
All inputs are finite; a program needn't handle non-finite values. No bound on the sum of `flags` on one device may be relied on, other than what follows from the above.
Results may differ from the reference program's by a relative error of at most 0.00065.
Values may be sent and summed in bfloat16 or wider, within the bound.
No kernel may reach another device: no remote copies, remote signals or barrier semaphores. Data moves between devices by JAX's collectives and lax.ppermute only.
A program may use at most 256 MiB of HBM per device.

```python
import math
import jax
import jax.numpy as jnp
from jax import lax

NI = 1024
NCH = 8192
TAPS = 4
CH_AVG = 64
SPECTRA = 16
SAMPLES = 262144
NOUT = 128
N_INP = 4


def draw_voltages(key, part):
    base = jax.random.fold_in(key, 17)
    key_shared, key_private = jax.random.split(base)
    shared = jax.random.randint(key_shared, (1, SAMPLES), -8, 8, dtype=jnp.int32)
    private = jax.random.randint(key_private, (NI, SAMPLES), -8, 8, dtype=jnp.int32)
    return shared + private


def place_ends(drawn, rng, smallest, top_value):
    longest = drawn.shape.index(max(drawn.shape))
    spots = []
    for shift in (0, 1):
        where = [jax.random.randint(jax.random.fold_in(rng, axis), (), 0, length) for axis, length in enumerate(drawn.shape)]
        where[longest] = (where[longest] + shift) % drawn.shape[longest]
        spots.append(tuple(where))
    return drawn.at[spots[0]].set(smallest).at[spots[1]].set(top_value)


def gaussian(own_key, shape, spread, most, kind=jnp.bfloat16):
    return jnp.clip(spread * jax.random.normal(own_key, shape, jnp.float32), -most, most).astype(kind)


def setup_inputs(seed: int = 0) -> dict:
    arg_keys = jax.random.split(jax.random.key(seed), 4)
    voltages = draw_voltages(jax.random.fold_in(arg_keys[3], 71), 0)
    taps = gaussian(arg_keys[1], (TAPS, 2 * NCH), 0.5, 3.0, jnp.float32)
    flags = place_ends((jax.random.randint(arg_keys[2], (NI,), 0, 8) < 7).astype(jnp.int32), jax.random.fold_in(arg_keys[2], 1), 0, 1)
    return {"voltages": voltages, "taps": taps, "flags": flags}


def reference(voltages, taps, flags):
    length = 2 * NCH
    block_inputs = math.gcd(NI, 64)
    block_count = NI // block_inputs
    blocked = voltages.reshape(block_count, block_inputs, SPECTRA, length)
    flag_blocks = flags.reshape(block_count, block_inputs)

    def filter_section(packed):
        raw_block, flag_block = packed
        samples = raw_block.astype(jnp.float32)
        padded = jnp.concatenate([samples, jnp.zeros((block_inputs, TAPS - 1, length), jnp.float32)], axis=1)
        filtered = jnp.zeros((block_inputs, SPECTRA, length), jnp.float32)
        for offset in range(TAPS):
            filtered = filtered + taps[offset][None, None, :] * padded[:, offset:offset + SPECTRA]
        transformed = jnp.fft.rfft(filtered, axis=-1)[..., :NCH]
        scale = flag_block.astype(jnp.float32)[:, None, None] / (8.0 * math.sqrt(length))
        stacked = jnp.stack([jnp.real(transformed) * scale, jnp.imag(transformed) * scale])
        return stacked.astype(jnp.bfloat16)
    spectra = lax.map(filter_section, (blocked, flag_blocks))
    spectra = jnp.transpose(spectra, (1, 0, 2, 3, 4)).reshape(2, NI, SPECTRA, NCH)
    norm = 1.0 / (SPECTRA * CH_AVG)
    highest = lax.Precision.HIGHEST

    def cross_section(group):
        start = (group * CH_AVG).astype(jnp.int32)
        segment = lax.dynamic_slice_in_dim(spectra, start, CH_AVG, 3).astype(jnp.float32)
        segment = segment.reshape(2, NI, SPECTRA * CH_AVG)
        real_rows = segment[0]
        imag_rows = segment[1]
        real_vis = jnp.dot(real_rows, real_rows.T, precision=highest) + jnp.dot(imag_rows, imag_rows.T, precision=highest)
        imag_vis = jnp.dot(imag_rows, real_rows.T, precision=highest) - jnp.dot(real_rows, imag_rows.T, precision=highest)
        return jnp.stack([real_vis, imag_vis]) * norm
    visibilities = lax.map(cross_section, jnp.arange(NOUT, dtype=jnp.int32))
    visibilities = jnp.transpose(visibilities, (1, 0, 2, 3))
    return visibilities.reshape(2, NOUT, N_INP, NI // N_INP, NI)
```

```python
import functools
import math

import jax
import jax.numpy as jnp
import ml_dtypes
import numpy as np
from jax import lax
from jax.experimental import pallas as pl
from jax.experimental.pallas import tpu as pltpu
from jax.sharding import PartitionSpec as P

CH_AVG = 64
LANES = 128
PAD = 136
F32 = jnp.float32
BF16 = jnp.bfloat16
VMEM_LIMIT = 56 * 1024 * 1024


def split_np(table):
    high = table.astype(np.float32).astype(ml_dtypes.bfloat16)
    low = (table - high.astype(np.float64)).astype(np.float32).astype(ml_dtypes.bfloat16)
    return high, low


def split(value):
    high = value.astype(BF16)
    return high, (value - high.astype(F32)).astype(BF16)


def angles(rows, columns, period):
    grid = np.arange(rows)[:, None] * np.arange(columns)[None, :]
    return (grid % period) * (2.0 * np.pi / period)


@functools.cache
def tables(length):
    first = angles(LANES, LANES, LANES)
    scale = 1.0 / (8.0 * math.sqrt(length))
    one = np.concatenate([np.cos(first), -np.sin(first)], axis=0) * scale
    high, low = split_np(one)
    table_one = np.concatenate(
        [
            np.concatenate([high, high], axis=1),
            np.concatenate([low, np.zeros_like(low)], axis=1),
        ],
        axis=0,
    )
    twist = angles(LANES, LANES, length)
    twists = np.stack([np.cos(twist), np.sin(twist)]).astype(np.float32)
    second = angles(LANES // 2, LANES, LANES)
    real = np.concatenate([np.cos(second), np.sin(second)], axis=1)
    imag = np.concatenate([-np.sin(second), np.cos(second)], axis=1)
    table_two = np.stack([np.stack(split_np(real)), np.stack(split_np(imag))], axis=1)
    return table_one, twists, table_two


def dft_kernel(items, length, deps, v_ref, taps_ref, flags_ref, one_ref, twist_ref, two_ref, *rest):
    outs = rest[deps:-2]
    samples, results = rest[-2:]
    rows = v_ref.shape[0]
    needed = sorted({s for item in items for _, s in item})

    @pl.loop(0, LANES, unroll=8)
    def _(n1):
        column = pl.multiple_of(n1 * LANES, LANES)
        taps = [taps_ref[k : k + 1, pl.ds(column, LANES)] for k in range(taps_ref.shape[0])]
        for part in range(rows // 8):
            v = {
                s: v_ref[part * 8 : part * 8 + 8, pl.ds(s * length + column, LANES)].astype(F32)
                for s in needed
            }
            for index, item in enumerate(items):
                total = None
                for k, s in item:
                    term = taps[k] * v[s]
                    total = term if total is None else total + term
                total = total * flags_ref[index, part * 8 : part * 8 + 8, :]
                start = (index * rows + part * 8) * PAD + n1
                samples[pl.ds(start, 8, stride=PAD), :] = total

    lower = lax.broadcasted_iota(jnp.int32, (LANES // 2, LANES), 1) < LANES // 2
    half = LANES // 2

    @pl.loop(0, len(items) * rows // 2, unroll=4)
    def _(pair):
        base = pl.multiple_of(pair * 2 * PAD, 8)
        data = jnp.concatenate(
            [samples[pl.ds(base, LANES), :], samples[pl.ds(base + PAD, LANES), :]], axis=1
        )
        high, low = split(data)
        y = jnp.dot(
            one_ref[...], jnp.concatenate([high, low], axis=0), preferred_element_type=F32
        )
        y = y[: 2 * LANES] + y[2 * LANES :]
        cos, sin = twist_ref[0], twist_ref[1]
        parts = []
        for e in range(2):
            real = y[:LANES, e * LANES : (e + 1) * LANES]
            imag = y[LANES:, e * LANES : (e + 1) * LANES]
            parts.append(
                jnp.concatenate([real * cos + imag * sin, imag * cos - real * sin], axis=1)
            )
        high, low = split(jnp.concatenate(parts, axis=0))
        dims = (((1,), (1,)), ((), ()))
        z = lax.dot_general(two_ref[...], high, dims, preferred_element_type=F32)
        z = z[:LANES] + z[LANES:]
        z = z + lax.dot_general(two_ref[:LANES, :], low, dims, preferred_element_type=F32)
        index = (pair * 2) // rows
        for e in range(2):
            row = pair * 2 + e - index * rows
            real = z[:half, e * LANES : (e + 1) * LANES]
            imag = z[half:, e * LANES : (e + 1) * LANES]
            even = jnp.where(lower, real, pltpu.roll(imag, half, 1))
            odd = jnp.where(lower, pltpu.roll(real, half, 1), imag)
            start = index * LANES * rows + row
            results[pl.ds(start, half, stride=2 * rows), :] = even
            results[pl.ds(start + rows, half, stride=2 * rows), :] = odd

    share = LANES * rows // len(outs)
    for to, out in enumerate(outs):
        for index in range(len(items)):
            chunk = results[pl.ds(index * LANES * rows + to * share, share), :]
            out[index] = chunk.astype(BF16).reshape(out.shape[1:])


def dft(items, voltages, taps, flags, one, twist, two, peers, blocks, part, parts, deps=()):
    inputs = voltages.shape[0] // parts
    length = taps.shape[1]
    rows = 16
    groups = LANES // (peers * blocks)
    count = len(items)
    whole = lambda shape: pl.BlockSpec(shape, lambda i: (0,) * len(shape))
    steps = inputs // rows
    out_shape = (count, blocks, groups, inputs, LANES)
    out_block = (count, blocks, groups, rows, LANES)
    return pl.pallas_call(
        functools.partial(dft_kernel, items, length, len(deps)),
        grid=(steps,),
        in_specs=[
            pl.BlockSpec((rows, voltages.shape[1]), lambda i: (i + part * steps, 0)),
            whole(taps.shape),
            pl.BlockSpec((count, rows, LANES), lambda i: (0, i + part * steps, 0)),
            whole(one.shape),
            whole(twist.shape),
            whole(two.shape),
        ]
        + [pl.BlockSpec(memory_space=pl.ANY)] * len(deps),
        out_specs=[pl.BlockSpec(out_block, lambda i: (0, 0, 0, i, 0))] * peers,
        out_shape=[jax.ShapeDtypeStruct(out_shape, BF16)] * peers,
        scratch_shapes=[
            pltpu.VMEM((count * rows * PAD, LANES), F32),
            pltpu.VMEM((count * rows * LANES, LANES), F32),
        ],
        compiler_params=pltpu.CompilerParams(vmem_limit_bytes=VMEM_LIMIT),
        cost_estimate=pl.CostEstimate(flops=0, bytes_accessed=1024, transcendentals=0),
        name="dft",
    )(voltages, taps, flags, one, twist, two, *deps)


def join_kernel(peers, partial, *refs):
    parts, out = refs[:peers], refs[-1]
    for e in range(peers):
        for z in range(out.shape[0]):
            value = parts[e][0, z]
            if partial:
                value = value.astype(F32) + parts[(e + 1) % peers][1, z].astype(F32)
            out[z, e] = value.astype(BF16)


def join(parts, partial, deps):
    peers = len(parts)
    count, blocks, groups, inputs, lanes = parts[0].shape
    step = inputs // 2 if inputs >= 32 else inputs
    shape = (blocks, peers, groups, inputs, lanes)
    return pl.pallas_call(
        functools.partial(join_kernel, peers, partial),
        grid=(inputs // step,),
        in_specs=[pl.BlockSpec(parts[0].shape[:3] + (step, lanes), lambda i: (0, 0, 0, i, 0))]
        * peers
        + [pl.BlockSpec(memory_space=pl.ANY)] * len(deps),
        out_specs=pl.BlockSpec(shape[:3] + (step, lanes), lambda i: (0, 0, 0, i, 0)),
        out_shape=jax.ShapeDtypeStruct(shape, BF16),
        compiler_params=pltpu.CompilerParams(vmem_limit_bytes=VMEM_LIMIT),
        cost_estimate=pl.CostEstimate(flops=10**11, bytes_accessed=1024, transcendentals=0),
        name="join",
    )(*parts, *deps)


def correlate_kernel(stages, parts, scale, add_to, place, *refs):
    count = stages * parts
    own, other = refs[:count], refs[count : 2 * count]
    rest = refs[2 * count :]
    before = rest[0] if add_to else None
    out, left, right = rest[-3:]
    blocks, times, some, lanes = own[0].shape
    inputs = some * parts
    core = place[0]
    lower = lax.broadcasted_iota(jnp.int32, (some, lanes), 1) < lanes // 2
    mine = pl.multiple_of(core * inputs, inputs)
    theirs = pl.multiple_of((1 - core) * inputs, inputs)
    for stage in range(stages):
        for part in range(parts):
            index = stage * parts + part
            row = part * some
            for z in range(blocks):
                for t in range(times):
                    column = slice((stage * times + t) * lanes, (stage * times + t + 1) * lanes)
                    tile = own[index][z, t]
                    left[z, row : row + some, column] = tile
                    turned = pltpu.roll(tile.astype(F32), lanes // 2, 1)
                    left[z, inputs + row : inputs + row + some, column] = jnp.where(
                        lower, turned, -turned
                    ).astype(BF16)
                    right[z, pl.ds(mine + row, some), column] = tile
                    right[z, pl.ds(theirs + row, some), column] = other[index][z, t]
    dims = (((1,), (1,)), ((), ()))
    for q in range(blocks):
        column = slice(q * 2 * inputs, (q + 1) * 2 * inputs)
        for a in range(blocks):
            block = lax.dot_general(left[a], right[q], dims, preferred_element_type=F32) * scale
            for part in range(2):
                value = block[part * inputs : (part + 1) * inputs]
                if add_to:
                    value = value + before[part, 0, a, :, column]
                out[part, 0, a, :, column] = value


def correlate(place, parts, own, other, scale, before=None):
    stages = len(own) // parts
    blocks, times, groups, some, lanes = own[0].shape
    inputs = some * parts
    depth = stages * times * lanes
    shape = (2, groups, blocks, inputs, 2 * blocks * inputs)
    arrays = own + other
    spec = pl.BlockSpec((blocks, times, None, some, lanes), lambda g: (0, 0, g, 0, 0))
    out_spec = pl.BlockSpec((2, 1) + shape[2:], lambda g: (0, g, 0, 0, 0))
    in_specs = [pl.BlockSpec(memory_space=pltpu.SMEM)] + [spec] * len(arrays)
    aliases = {}
    if before is not None:
        in_specs.append(out_spec)
        arrays = arrays + [before]
        aliases = {len(arrays): 0}
    return pl.pallas_call(
        functools.partial(correlate_kernel, stages, parts, scale, before is not None),
        grid=(groups,),
        in_specs=in_specs,
        out_specs=out_spec,
        out_shape=jax.ShapeDtypeStruct(shape, F32),
        scratch_shapes=[pltpu.VMEM((blocks, 2 * inputs, depth), BF16)] * 2,
        input_output_aliases=aliases,
        compiler_params=pltpu.CompilerParams(vmem_limit_bytes=VMEM_LIMIT),
        cost_estimate=pl.CostEstimate(
            flops=2 * math.prod(shape) * depth,
            bytes_accessed=math.prod(shape) * 4 * (1 if before is None else 2),
            transcendentals=0,
        ),
        name="correlate",
    )(place, *arrays)


def shift(value, axis, step):
    count = lax.axis_size(axis)
    return lax.ppermute(value, axis, [(i, (i + step) % count) for i in range(count)])


def turn(value, axis):
    return lax.all_to_all(value, axis, split_axis=0, concat_axis=0, tiled=True)


def shards(voltages, taps, flags):
    length = taps.shape[1]
    reach = taps.shape[0]
    spectra = voltages.shape[1] // length
    parts = 2
    blocks, peers = lax.axis_size("inp"), lax.axis_size("tm")
    t, core = lax.axis_index("tm"), lax.axis_index("bl")
    table_one, twists, table_two = tables(length)
    place = jnp.stack([core]).astype(jnp.int32)

    per = LANES // 2 // (blocks * peers)
    home_t = (t + jnp.arange(peers, dtype=jnp.int32)) % peers
    home_z = jnp.arange(blocks, dtype=jnp.int32)
    order = (home_z[None, :] * peers + home_t[:, None])[:, :, None] * per
    order = (order + jnp.arange(per, dtype=jnp.int32)).reshape(-1)
    two = jnp.take(jnp.asarray(table_two), order, axis=2).reshape(2 * LANES, 2 * LANES)
    one, twist = jnp.asarray(table_one), jnp.asarray(twists)

    keep = jnp.broadcast_to(flags.astype(F32)[:, None], (flags.shape[0], LANES))
    keep_two = jnp.stack([keep, keep * (t > 0).astype(F32)])

    work = [(j, part) for j in range(spectra) for part in range(parts)]
    from_dft, own, other = {}, {}, {}
    last = []

    def partial(c):
        return work[c][0] + reach > spectra

    def do_dft(c):
        j, part = work[c]
        items = [[(k, j + k) for k in range(reach) if j + k < spectra]]
        if partial(c):
            items.append([(k, j + k - spectra) for k in range(reach) if j + k >= spectra])
        sent = dft(
            items, voltages, taps, keep_two[: len(items)], one, twist, two, peers, blocks,
            part, parts, last,
        )
        last[:] = [sent[0]]
        got = {d: shift(sent[d], "tm", d) for d in range(1, peers)}
        from_dft[c] = [sent[0]] + [got[peers - e] for e in range(1, peers)]

    def do_join(c):
        early = [own[c - 2]] if c >= 2 else []
        early += [other[c - 3]] if c >= 3 else []
        sent = join(from_dft[c], partial(c), last + early)
        last[:] = [sent]
        own[c] = turn(sent, "inp")
        other[c] = shift(own[c], "bl", 1)

    count = len(work)
    for c in range(count + 1):
        if c < count:
            do_dft(c)
        if c >= 1:
            do_join(c - 1)

    def chunks(first, end):
        return [own[c] for c in range(first, end)], [other[c] for c in range(first, end)]

    scale = 1.0 / (peers * spectra * CH_AVG)
    before = correlate(place, parts, *chunks(0, count - parts), scale)
    return correlate(place, parts, *chunks(count - parts, count), scale, before)


def solution(mesh):
    in_specs = (P(("inp", "bl"), "tm"), P(), P(("inp", "bl")))
    out_specs = P(None, ("inp", "tm"), None, "bl", None)
    return jax.shard_map(shards, mesh=mesh, in_specs=in_specs, out_specs=out_specs, check_vma=False)
```

```python
import functools
import math

import jax
import jax.numpy as jnp
import ml_dtypes
import numpy as np
from jax import lax
from jax.experimental import pallas as pl
from jax.experimental.pallas import tpu as pltpu
from jax.sharding import PartitionSpec as P

CH_AVG = 64
LANES = 128
PAD = 136
F32 = jnp.float32
BF16 = jnp.bfloat16
VMEM_LIMIT = 56 * 1024 * 1024


def split_np(table):
    high = table.astype(np.float32).astype(ml_dtypes.bfloat16)
    low = (table - high.astype(np.float64)).astype(np.float32).astype(ml_dtypes.bfloat16)
    return high, low


def split(value):
    high = value.astype(BF16)
    return high, (value - high.astype(F32)).astype(BF16)


def angles(rows, columns, period):
    grid = np.arange(rows)[:, None] * np.arange(columns)[None, :]
    return (grid % period) * (2.0 * np.pi / period)


@functools.cache
def tables(length):
    first = angles(LANES, LANES, LANES)
    scale = 1.0 / (8.0 * math.sqrt(length))
    one = np.concatenate([np.cos(first), -np.sin(first)], axis=0) * scale
    high, low = split_np(one)
    table_one = np.concatenate(
        [
            np.concatenate([high, high], axis=1),
            np.concatenate([low, np.zeros_like(low)], axis=1),
        ],
        axis=0,
    )
    twist = angles(LANES, LANES, length)
    twists = np.stack([np.cos(twist), np.sin(twist)]).astype(np.float32)
    second = angles(LANES // 2, LANES, LANES)
    real = np.concatenate([np.cos(second), np.sin(second)], axis=1)
    imag = np.concatenate([-np.sin(second), np.cos(second)], axis=1)
    table_two = np.stack([np.stack(split_np(real)), np.stack(split_np(imag))], axis=1)
    return table_one, twists, table_two


def dft_kernel(items, length, deps, v_ref, taps_ref, flags_ref, one_ref, twist_ref, two_ref, *rest):
    outs = rest[deps:-2]
    samples, results = rest[-2:]
    rows = v_ref.shape[0]
    needed = sorted({s for item in items for _, s in item})

    @pl.loop(0, LANES, unroll=8)
    def _(n1):
        column = pl.multiple_of(n1 * LANES, LANES)
        taps = [taps_ref[k : k + 1, pl.ds(column, LANES)] for k in range(taps_ref.shape[0])]
        for part in range(rows // 8):
            v = {
                s: v_ref[part * 8 : part * 8 + 8, pl.ds(s * length + column, LANES)].astype(F32)
                for s in needed
            }
            for index, item in enumerate(items):
                total = None
                for k, s in item:
                    term = taps[k] * v[s]
                    total = term if total is None else total + term
                total = total * flags_ref[index, part * 8 : part * 8 + 8, :]
                start = (index * rows + part * 8) * PAD + n1
                samples[pl.ds(start, 8, stride=PAD), :] = total

    lower = lax.broadcasted_iota(jnp.int32, (LANES // 2, LANES), 1) < LANES // 2
    half = LANES // 2

    @pl.loop(0, len(items) * rows // 2, unroll=4)
    def _(pair):
        base = pl.multiple_of(pair * 2 * PAD, 8)
        data = jnp.concatenate(
            [samples[pl.ds(base, LANES), :], samples[pl.ds(base + PAD, LANES), :]], axis=1
        )
        high, low = split(data)
        y = jnp.dot(
            one_ref[...], jnp.concatenate([high, low], axis=0), preferred_element_type=F32
        )
        y = y[: 2 * LANES] + y[2 * LANES :]
        cos, sin = twist_ref[0], twist_ref[1]
        parts = []
        for e in range(2):
            real = y[:LANES, e * LANES : (e + 1) * LANES]
            imag = y[LANES:, e * LANES : (e + 1) * LANES]
            parts.append(
                jnp.concatenate([real * cos + imag * sin, imag * cos - real * sin], axis=1)
            )
        high, low = split(jnp.concatenate(parts, axis=0))
        dims = (((1,), (1,)), ((), ()))
        z = lax.dot_general(two_ref[...], high, dims, preferred_element_type=F32)
        z = z[:LANES] + z[LANES:]
        z = z + lax.dot_general(two_ref[:LANES, :], low, dims, preferred_element_type=F32)
        index = (pair * 2) // rows
        for e in range(2):
            row = pair * 2 + e - index * rows
            real = z[:half, e * LANES : (e + 1) * LANES]
            imag = z[half:, e * LANES : (e + 1) * LANES]
            even = jnp.where(lower, real, pltpu.roll(imag, half, 1))
            odd = jnp.where(lower, pltpu.roll(real, half, 1), imag)
            start = index * LANES * rows + row
            results[pl.ds(start, half, stride=2 * rows), :] = even
            results[pl.ds(start + rows, half, stride=2 * rows), :] = odd

    share = LANES * rows // len(outs)
    for to, out in enumerate(outs):
        for index in range(len(items)):
            chunk = results[pl.ds(index * LANES * rows + to * share, share), :]
            out[index] = chunk.astype(BF16).reshape(out.shape[1:])


def dft(items, voltages, taps, flags, one, twist, two, peers, blocks, part, parts, deps=()):
    inputs = voltages.shape[0] // parts
    length = taps.shape[1]
    rows = 16
    groups = LANES // (peers * blocks)
    count = len(items)
    whole = lambda shape: pl.BlockSpec(shape, lambda i: (0,) * len(shape))
    steps = inputs // rows
    out_shape = (count, blocks, groups, inputs, LANES)
    out_block = (count, blocks, groups, rows, LANES)
    return pl.pallas_call(
        functools.partial(dft_kernel, items, length, len(deps)),
        grid=(steps,),
        in_specs=[
            pl.BlockSpec((rows, voltages.shape[1]), lambda i: (i + part * steps, 0)),
            whole(taps.shape),
            pl.BlockSpec((count, rows, LANES), lambda i: (0, i + part * steps, 0)),
            whole(one.shape),
            whole(twist.shape),
            whole(two.shape),
        ]
        + [pl.BlockSpec(memory_space=pl.ANY)] * len(deps),
        out_specs=[pl.BlockSpec(out_block, lambda i: (0, 0, 0, i, 0))] * peers,
        out_shape=[jax.ShapeDtypeStruct(out_shape, BF16)] * peers,
        scratch_shapes=[
            pltpu.VMEM((count * rows * PAD, LANES), F32),
            pltpu.VMEM((count * rows * LANES, LANES), F32),
        ],
        compiler_params=pltpu.CompilerParams(vmem_limit_bytes=VMEM_LIMIT),
        cost_estimate=pl.CostEstimate(flops=0, bytes_accessed=1024, transcendentals=0),
        name="dft",
    )(voltages, taps, flags, one, twist, two, *deps)


def join_kernel(peers, partial, *refs):
    parts, out = refs[:peers], refs[-1]
    for e in range(peers):
        for z in range(out.shape[0]):
            value = parts[e][0, z]
            if partial:
                value = value.astype(F32) + parts[(e + 1) % peers][1, z].astype(F32)
            out[z, e] = value.astype(BF16)


def join(parts, partial, deps):
    peers = len(parts)
    count, blocks, groups, inputs, lanes = parts[0].shape
    step = inputs // 2 if inputs >= 32 else inputs
    shape = (blocks, peers, groups, inputs, lanes)
    return pl.pallas_call(
        functools.partial(join_kernel, peers, partial),
        grid=(inputs // step,),
        in_specs=[pl.BlockSpec(parts[0].shape[:3] + (step, lanes), lambda i: (0, 0, 0, i, 0))]
        * peers
        + [pl.BlockSpec(memory_space=pl.ANY)] * len(deps),
        out_specs=pl.BlockSpec(shape[:3] + (step, lanes), lambda i: (0, 0, 0, i, 0)),
        out_shape=jax.ShapeDtypeStruct(shape, BF16),
        compiler_params=pltpu.CompilerParams(vmem_limit_bytes=VMEM_LIMIT),
        cost_estimate=pl.CostEstimate(flops=28 * 10**9, bytes_accessed=1024, transcendentals=0),
        name="join",
    )(*parts, *deps)


def correlate_kernel(stages, parts, scale, add_to, place, *refs):
    count = stages * parts
    own, other = refs[:count], refs[count : 2 * count]
    rest = refs[2 * count :]
    before = rest[0] if add_to else None
    out, left, right = rest[-3:]
    blocks, times, some, lanes = own[0].shape
    inputs = some * parts
    core = place[0]
    lower = lax.broadcasted_iota(jnp.int32, (some, lanes), 1) < lanes // 2
    mine = pl.multiple_of(core * inputs, inputs)
    theirs = pl.multiple_of((1 - core) * inputs, inputs)
    for stage in range(stages):
        for part in range(parts):
            index = stage * parts + part
            row = part * some
            for z in range(blocks):
                for t in range(times):
                    column = slice((stage * times + t) * lanes, (stage * times + t + 1) * lanes)
                    tile = own[index][z, t]
                    left[z, row : row + some, column] = tile
                    turned = pltpu.roll(tile.astype(F32), lanes // 2, 1)
                    left[z, inputs + row : inputs + row + some, column] = jnp.where(
                        lower, turned, -turned
                    ).astype(BF16)
                    right[z, pl.ds(mine + row, some), column] = tile
                    right[z, pl.ds(theirs + row, some), column] = other[index][z, t]
    dims = (((1,), (1,)), ((), ()))
    for q in range(blocks):
        column = slice(q * 2 * inputs, (q + 1) * 2 * inputs)
        for a in range(blocks):
            block = lax.dot_general(left[a], right[q], dims, preferred_element_type=F32) * scale
            for part in range(2):
                value = block[part * inputs : (part + 1) * inputs]
                if add_to:
                    value = value + before[part, 0, a, :, column]
                out[part, 0, a, :, column] = value


def correlate(place, parts, own, other, scale, before=None):
    stages = len(own) // parts
    blocks, times, groups, some, lanes = own[0].shape
    inputs = some * parts
    depth = stages * times * lanes
    shape = (2, groups, blocks, inputs, 2 * blocks * inputs)
    arrays = own + other
    spec = pl.BlockSpec((blocks, times, None, some, lanes), lambda g: (0, 0, g, 0, 0))
    out_spec = pl.BlockSpec((2, 1) + shape[2:], lambda g: (0, g, 0, 0, 0))
    in_specs = [pl.BlockSpec(memory_space=pltpu.SMEM)] + [spec] * len(arrays)
    aliases = {}
    if before is not None:
        in_specs.append(out_spec)
        arrays = arrays + [before]
        aliases = {len(arrays): 0}
    return pl.pallas_call(
        functools.partial(correlate_kernel, stages, parts, scale, before is not None),
        grid=(groups,),
        in_specs=in_specs,
        out_specs=out_spec,
        out_shape=jax.ShapeDtypeStruct(shape, F32),
        scratch_shapes=[pltpu.VMEM((blocks, 2 * inputs, depth), BF16)] * 2,
        input_output_aliases=aliases,
        compiler_params=pltpu.CompilerParams(vmem_limit_bytes=VMEM_LIMIT),
        cost_estimate=pl.CostEstimate(
            flops=2 * math.prod(shape) * depth,
            bytes_accessed=math.prod(shape) * 4 * (1 if before is None else 2),
            transcendentals=0,
        ),
        name="correlate",
    )(place, *arrays)


def after(values, dep):
    count = len(values)
    anywhere = pl.BlockSpec(memory_space=pl.ANY)
    return pl.pallas_call(
        lambda *refs: None,
        in_specs=[anywhere] * (count + 1),
        out_specs=[anywhere] * count,
        out_shape=[jax.ShapeDtypeStruct(x.shape, x.dtype) for x in values],
        input_output_aliases={i: i for i in range(count)},
        name="after",
    )(*values, dep)


def shift(value, axis, step):
    count = lax.axis_size(axis)
    return lax.ppermute(value, axis, [(i, (i + step) % count) for i in range(count)])


def turn(value, axis):
    return lax.all_to_all(value, axis, split_axis=0, concat_axis=0, tiled=True)


def shards(voltages, taps, flags):
    length = taps.shape[1]
    reach = taps.shape[0]
    spectra = voltages.shape[1] // length
    parts = 2
    blocks, peers = lax.axis_size("inp"), lax.axis_size("tm")
    t, core = lax.axis_index("tm"), lax.axis_index("bl")
    table_one, twists, table_two = tables(length)
    place = jnp.stack([core]).astype(jnp.int32)

    per = LANES // 2 // (blocks * peers)
    home_t = (t + jnp.arange(peers, dtype=jnp.int32)) % peers
    home_z = jnp.arange(blocks, dtype=jnp.int32)
    order = (home_z[None, :] * peers + home_t[:, None])[:, :, None] * per
    order = (order + jnp.arange(per, dtype=jnp.int32)).reshape(-1)
    two = jnp.take(jnp.asarray(table_two), order, axis=2).reshape(2 * LANES, 2 * LANES)
    one, twist = jnp.asarray(table_one), jnp.asarray(twists)

    keep = jnp.broadcast_to(flags.astype(F32)[:, None], (flags.shape[0], LANES))
    keep_two = jnp.stack([keep, keep * (t > 0).astype(F32)])

    work = [(j, part) for j in range(spectra) for part in range(parts)]
    from_dft, own, other = {}, {}, {}
    last = []

    def partial(c):
        return work[c][0] + reach > spectra

    def do_dft(c):
        j, part = work[c]
        items = [[(k, j + k) for k in range(reach) if j + k < spectra]]
        if partial(c):
            items.append([(k, j + k - spectra) for k in range(reach) if j + k >= spectra])
        sent = dft(
            items, voltages, taps, keep_two[: len(items)], one, twist, two, peers, blocks,
            part, parts, last,
        )
        last[:] = [sent[0]]
        got = {d: shift(sent[d], "tm", d) for d in range(1, peers)}
        from_dft[c] = [sent[0]] + [got[peers - e] for e in range(1, peers)]

    def do_join(c):
        early = [own[c - 2]] if c >= 2 else []
        early += [other[c - 3]] if c >= 3 else []
        sent = join(from_dft[c], partial(c), last + early)
        last[:] = [sent]
        own[c] = turn(sent, "inp")
        other[c] = shift(own[c], "bl", 1)

    count = len(work)
    for c in range(count + 1):
        if c < count:
            do_dft(c)
        if c >= 1:
            do_join(c - 1)

    scale = 1.0 / (peers * spectra * CH_AVG)
    early, late = range(count - parts), range(count - parts, count)
    before = correlate(
        place, parts, [own[c] for c in early], [other[c] for c in early], scale
    )
    own[count - 1] = after([own[count - 1]], before)[0]
    other[count - 1] = shift(own[count - 1], "bl", 1)
    return correlate(
        place, parts, [own[c] for c in late], [other[c] for c in late], scale, before
    )


def solution(mesh):
    in_specs = (P(("inp", "bl"), "tm"), P(), P(("inp", "bl")))
    out_specs = P(None, ("inp", "tm"), None, "bl", None)
    return jax.shard_map(shards, mesh=mesh, in_specs=in_specs, out_specs=out_specs, check_vma=False)
```

```python
import functools
import math

import jax
import jax.numpy as jnp
import ml_dtypes
import numpy as np
from jax import lax
from jax.experimental import pallas as pl
from jax.experimental.pallas import tpu as pltpu
from jax.sharding import PartitionSpec as P

CH_AVG = 64
LANES = 128
PAD = 136
F32 = jnp.float32
BF16 = jnp.bfloat16
VMEM_LIMIT = 56 * 1024 * 1024


def split_np(table):
    high = table.astype(np.float32).astype(ml_dtypes.bfloat16)
    low = (table - high.astype(np.float64)).astype(np.float32).astype(ml_dtypes.bfloat16)
    return high, low


def split(value):
    high = value.astype(BF16)
    return high, (value - high.astype(F32)).astype(BF16)


def angles(rows, columns, period):
    grid = np.arange(rows)[:, None] * np.arange(columns)[None, :]
    return (grid % period) * (2.0 * np.pi / period)


@functools.cache
def tables(length):
    first = angles(LANES, LANES, LANES)
    scale = 1.0 / (8.0 * math.sqrt(length))
    one = np.concatenate([np.cos(first), -np.sin(first)], axis=0) * scale
    high, low = split_np(one)
    table_one = np.concatenate(
        [
            np.concatenate([high, high], axis=1),
            np.concatenate([low, np.zeros_like(low)], axis=1),
        ],
        axis=0,
    )
    twist = angles(LANES, LANES, length)
    twists = np.stack([np.cos(twist), np.sin(twist)]).astype(np.float32)
    second = angles(LANES // 2, LANES, LANES)
    real = np.concatenate([np.cos(second), np.sin(second)], axis=1)
    imag = np.concatenate([-np.sin(second), np.cos(second)], axis=1)
    table_two = np.stack([np.stack(split_np(real)), np.stack(split_np(imag))], axis=1)
    return table_one, twists, table_two


def dft_kernel(items, length, deps, place, v_ref, taps_ref, flags_ref, one_ref, twist_ref, two_ref, *rest):
    outs = rest[deps:-2]
    samples, results = rest[-2:]
    rows = v_ref.shape[0]
    needed = sorted({s for item in items for _, s in item})

    @pl.loop(0, LANES, unroll=8)
    def _(n1):
        column = pl.multiple_of(n1 * LANES, LANES)
        taps = [taps_ref[k : k + 1, pl.ds(column, LANES)] for k in range(taps_ref.shape[0])]
        for part in range(rows // 8):
            v = {
                s: v_ref[part * 8 : part * 8 + 8, pl.ds(s * length + column, LANES)].astype(F32)
                for s in needed
            }
            for index, item in enumerate(items):
                total = None
                for k, s in item:
                    term = taps[k] * v[s]
                    total = term if total is None else total + term
                total = total * flags_ref[index, part * 8 : part * 8 + 8, :]
                start = (index * rows + part * 8) * PAD + n1
                samples[pl.ds(start, 8, stride=PAD), :] = total

    lower = lax.broadcasted_iota(jnp.int32, (LANES // 2, LANES), 1) < LANES // 2
    half = LANES // 2

    @pl.loop(0, len(items) * rows // 2, unroll=8)
    def _(pair):
        base = pl.multiple_of(pair * 2 * PAD, 8)
        data = jnp.concatenate(
            [samples[pl.ds(base, LANES), :], samples[pl.ds(base + PAD, LANES), :]], axis=1
        )
        high, low = split(data)
        y = jnp.dot(
            one_ref[...], jnp.concatenate([high, low], axis=0), preferred_element_type=F32
        )
        y = y[: 2 * LANES] + y[2 * LANES :]
        cos, sin = twist_ref[0], twist_ref[1]
        parts = []
        for e in range(2):
            real = y[:LANES, e * LANES : (e + 1) * LANES]
            imag = y[LANES:, e * LANES : (e + 1) * LANES]
            parts.append(
                jnp.concatenate([real * cos + imag * sin, imag * cos - real * sin], axis=1)
            )
        high, low = split(jnp.concatenate(parts, axis=0))
        dims = (((1,), (1,)), ((), ()))
        z = lax.dot_general(two_ref[...], high, dims, preferred_element_type=F32)
        z = z[:LANES] + z[LANES:]
        z = z + lax.dot_general(two_ref[:LANES, :], low, dims, preferred_element_type=F32)
        index = (pair * 2) // rows
        for e in range(2):
            row = pair * 2 + e - index * rows
            real = z[:half, e * LANES : (e + 1) * LANES]
            imag = z[half:, e * LANES : (e + 1) * LANES]
            even = jnp.where(lower, real, pltpu.roll(imag, half, 1))
            odd = jnp.where(lower, pltpu.roll(real, half, 1), imag)
            start = index * LANES * rows + row
            results[pl.ds(start, half, stride=2 * rows), :] = even
            results[pl.ds(start + rows, half, stride=2 * rows), :] = odd

    share = LANES * rows // len(outs)
    for step, out in enumerate(outs):
        home = lax.rem(place[1] + step, len(outs))
        for index in range(len(items)):
            start = pl.multiple_of(index * LANES * rows + home * share, share)
            out[index] = results[pl.ds(start, share), :].astype(BF16).reshape(out.shape[1:])


def dft(items, place, voltages, taps, flags, one, twist, two, peers, blocks, part, parts, deps=()):
    inputs = voltages.shape[0] // parts
    length = taps.shape[1]
    rows = 16
    groups = LANES // (peers * blocks)
    count = len(items)
    whole = lambda shape: pl.BlockSpec(shape, lambda i: (0,) * len(shape))
    steps = inputs // rows
    out_shape = (count, blocks, groups, inputs, LANES)
    out_block = (count, blocks, groups, rows, LANES)
    return pl.pallas_call(
        functools.partial(dft_kernel, items, length, len(deps)),
        grid=(steps,),
        in_specs=[
            pl.BlockSpec(memory_space=pltpu.SMEM),
            pl.BlockSpec((rows, voltages.shape[1]), lambda i: (i + part * steps, 0)),
            whole(taps.shape),
            pl.BlockSpec((count, rows, LANES), lambda i: (0, i + part * steps, 0)),
            whole(one.shape),
            whole(twist.shape),
            whole(two.shape),
        ]
        + [pl.BlockSpec(memory_space=pl.ANY)] * len(deps),
        out_specs=[pl.BlockSpec(out_block, lambda i: (0, 0, 0, i, 0))] * peers,
        out_shape=[jax.ShapeDtypeStruct(out_shape, BF16)] * peers,
        scratch_shapes=[
            pltpu.VMEM((count * rows * PAD, LANES), F32),
            pltpu.VMEM((count * rows * LANES, LANES), F32),
        ],
        compiler_params=pltpu.CompilerParams(vmem_limit_bytes=VMEM_LIMIT),
        cost_estimate=pl.CostEstimate(flops=0, bytes_accessed=1024, transcendentals=0),
        name="dft",
    )(place, voltages, taps, flags, one, twist, two, *deps)


def join_kernel(peers, partial, *refs):
    parts, out = refs[:peers], refs[-1]
    for e in range(peers):
        for z in range(out.shape[0]):
            value = parts[e][0, z]
            if partial:
                value = value.astype(F32) + parts[(e + 1) % peers][1, z].astype(F32)
            out[z, e] = value.astype(BF16)


def join(parts, partial, deps):
    peers = len(parts)
    count, blocks, groups, inputs, lanes = parts[0].shape
    step = inputs // 2 if inputs >= 32 else inputs
    shape = (blocks, peers, groups, inputs, lanes)
    return pl.pallas_call(
        functools.partial(join_kernel, peers, partial),
        grid=(inputs // step,),
        in_specs=[pl.BlockSpec(parts[0].shape[:3] + (step, lanes), lambda i: (0, 0, 0, i, 0))]
        * peers
        + [pl.BlockSpec(memory_space=pl.ANY)] * len(deps),
        out_specs=pl.BlockSpec(shape[:3] + (step, lanes), lambda i: (0, 0, 0, i, 0)),
        out_shape=jax.ShapeDtypeStruct(shape, BF16),
        compiler_params=pltpu.CompilerParams(vmem_limit_bytes=VMEM_LIMIT),
        cost_estimate=pl.CostEstimate(flops=28 * 10**9, bytes_accessed=1024, transcendentals=0),
        name="join",
    )(*parts, *deps)


def correlate_kernel(stages, parts, scale, add_to, place, *refs):
    count = stages * parts
    own, other = refs[:count], refs[count : 2 * count]
    rest = refs[2 * count :]
    before = rest[0] if add_to else None
    out, left, right = rest[-3:]
    blocks, times, some, lanes = own[0].shape
    inputs = some * parts
    core = place[0]
    lower = lax.broadcasted_iota(jnp.int32, (some, lanes), 1) < lanes // 2
    mine = pl.multiple_of(core * inputs, inputs)
    theirs = pl.multiple_of((1 - core) * inputs, inputs)
    for stage in range(stages):
        for part in range(parts):
            index = stage * parts + part
            row = part * some
            for z in range(blocks):
                for t in range(times):
                    column = slice((stage * times + t) * lanes, (stage * times + t + 1) * lanes)
                    tile = own[index][z, t]
                    left[z, row : row + some, column] = tile
                    turned = pltpu.roll(tile.astype(F32), lanes // 2, 1)
                    left[z, inputs + row : inputs + row + some, column] = jnp.where(
                        lower, turned, -turned
                    ).astype(BF16)
                    right[z, pl.ds(mine + row, some), column] = tile
                    right[z, pl.ds(theirs + row, some), column] = other[index][z, t]
    dims = (((1,), (1,)), ((), ()))
    for q in range(blocks):
        column = slice(q * 2 * inputs, (q + 1) * 2 * inputs)
        for a in range(blocks):
            block = lax.dot_general(left[a], right[q], dims, preferred_element_type=F32) * scale
            for part in range(2):
                value = block[part * inputs : (part + 1) * inputs]
                if add_to:
                    value = value + before[part, 0, a, :, column]
                out[part, 0, a, :, column] = value


def correlate(place, parts, own, other, scale, before=None):
    stages = len(own) // parts
    blocks, times, groups, some, lanes = own[0].shape
    inputs = some * parts
    depth = stages * times * lanes
    shape = (2, groups, blocks, inputs, 2 * blocks * inputs)
    arrays = own + other
    spec = pl.BlockSpec((blocks, times, None, some, lanes), lambda g: (0, 0, g, 0, 0))
    out_spec = pl.BlockSpec((2, 1) + shape[2:], lambda g: (0, g, 0, 0, 0))
    in_specs = [pl.BlockSpec(memory_space=pltpu.SMEM)] + [spec] * len(arrays)
    aliases = {}
    if before is not None:
        in_specs.append(out_spec)
        arrays = arrays + [before]
        aliases = {len(arrays): 0}
    return pl.pallas_call(
        functools.partial(correlate_kernel, stages, parts, scale, before is not None),
        grid=(groups,),
        in_specs=in_specs,
        out_specs=out_spec,
        out_shape=jax.ShapeDtypeStruct(shape, F32),
        scratch_shapes=[pltpu.VMEM((blocks, 2 * inputs, depth), BF16)] * 2,
        input_output_aliases=aliases,
        compiler_params=pltpu.CompilerParams(vmem_limit_bytes=VMEM_LIMIT),
        cost_estimate=pl.CostEstimate(
            flops=2 * math.prod(shape) * depth,
            bytes_accessed=math.prod(shape) * 4 * (1 if before is None else 2),
            transcendentals=0,
        ),
        name="correlate",
    )(place, *arrays)


def after(values, dep):
    count = len(values)
    anywhere = pl.BlockSpec(memory_space=pl.ANY)
    return pl.pallas_call(
        lambda *refs: None,
        in_specs=[anywhere] * (count + 1),
        out_specs=[anywhere] * count,
        out_shape=[jax.ShapeDtypeStruct(x.shape, x.dtype) for x in values],
        input_output_aliases={i: i for i in range(count)},
        name="after",
    )(*values, dep)


def shift(value, axis, step):
    count = lax.axis_size(axis)
    return lax.ppermute(value, axis, [(i, (i + step) % count) for i in range(count)])


def turn(value, axis):
    return lax.all_to_all(value, axis, split_axis=0, concat_axis=0, tiled=True)


def shards(voltages, taps, flags):
    length = taps.shape[1]
    reach = taps.shape[0]
    spectra = voltages.shape[1] // length
    parts = 2
    blocks, peers = lax.axis_size("inp"), lax.axis_size("tm")
    t, core = lax.axis_index("tm"), lax.axis_index("bl")
    table_one, twists, table_two = tables(length)
    place = jnp.stack([core, t]).astype(jnp.int32)

    per = LANES // 2 // (blocks * peers)
    order = np.arange(LANES // 2).reshape(blocks, peers, per).transpose(1, 0, 2).reshape(-1)
    two = jnp.asarray(table_two[:, :, order].reshape(2 * LANES, 2 * LANES))
    one, twist = jnp.asarray(table_one), jnp.asarray(twists)

    keep = jnp.broadcast_to(flags.astype(F32)[:, None], (flags.shape[0], LANES))
    keep_two = jnp.stack([keep, keep * (t > 0).astype(F32)])

    work = [(j, part) for j in range(spectra) for part in range(parts)]
    from_dft, own, other = {}, {}, {}
    last = []

    def partial(c):
        return work[c][0] + reach > spectra

    def do_dft(c):
        j, part = work[c]
        items = [[(k, j + k) for k in range(reach) if j + k < spectra]]
        if partial(c):
            items.append([(k, j + k - spectra) for k in range(reach) if j + k >= spectra])
        sent = dft(
            items, place, voltages, taps, keep_two[: len(items)], one, twist, two, peers, blocks,
            part, parts, last,
        )
        last[:] = [sent[0]]
        got = {d: shift(sent[d], "tm", d) for d in range(1, peers)}
        from_dft[c] = [sent[0]] + [got[peers - e] for e in range(1, peers)]

    def do_join(c):
        early = [own[c - 2]] if c >= 2 else []
        early += [other[c - 3]] if c >= 3 else []
        sent = join(from_dft[c], partial(c), last + early)
        last[:] = [sent]
        own[c] = turn(sent, "inp")
        other[c] = shift(own[c], "bl", 1)

    count = len(work)
    for c in range(count + 1):
        if c < count:
            do_dft(c)
        if c >= 1:
            do_join(c - 1)

    scale = 1.0 / (peers * spectra * CH_AVG)
    early, late = range(count - parts), range(count - parts, count)
    before = correlate(
        place, parts, [own[c] for c in early], [other[c] for c in early], scale
    )
    own[count - 1] = after([own[count - 1]], before)[0]
    other[count - 1] = shift(own[count - 1], "bl", 1)
    return correlate(
        place, parts, [own[c] for c in late], [other[c] for c in late], scale, before
    )


def solution(mesh):
    in_specs = (P(("inp", "bl"), "tm"), P(), P(("inp", "bl")))
    out_specs = P(None, ("inp", "tm"), None, "bl", None)
    return jax.shard_map(shards, mesh=mesh, in_specs=in_specs, out_specs=out_specs, check_vma=False)
```
